32 devices in a mesh: seq: 8 (over z, core), chan: 4 (over y, x).
Axes of the slice: x: 2, y: 2, z: 4, core: 2. Of those that a mesh axis runs over, the one named last changes fastest.
Arguments:
- layer_source: bfloat16 [8192, 4096], P('seq', 'chan'), may hold values from -6 to 6
- entering_mixer_sections: bfloat16 [2, 8192, 1024], P(None, 'chan'), may hold values from -0.125 to 0.125
- sigmoid_switch_matrix: bfloat16 [4096, 1024], P('chan'), may hold values from -0.1875 to 0.1875
- leaving_mixer_sections: bfloat16 [2, 8192, 1024], P(None, 'chan'), may hold values from -0.125 to 0.125
- channel_persistence: float32 [4096], P('chan'), may hold values from 0.96 to 1, as said below
- position_boosts: float32 [8192], P('seq'), may hold values from 0.5 to 1, as said below
- result_cotangent: bfloat16 [8192, 4096], P('seq', 'chan'), may hold values from -6 to 6
Outputs:
- layer_out: bfloat16 [8192, 4096], P('seq', 'chan')
- token_grads: bfloat16 [8192, 4096], P('seq', 'chan')
- in_grads: float32 [2, 8192, 1024], P(None, ('chan', 'seq'))
- out_grads: float32 [2, 8192, 1024], P(None, ('chan', 'seq'))
- gate_grads: float32 [4096, 1024], P(('chan', 'seq'))
The draws below stay inside these ranges and needn't reach their ends.
Inputs may be any that keep to these rules, and one draw needn't show every extreme that they name: `channel_persistence`: each entry is positive and below one. `position_boosts`: each entry is positive and at most one.
All inputs are finite; a program needn't handle non-finite values.
Results may differ from the reference program's by a relative error of at most 0.027.
Values may be sent and summed in bfloat16 or wider, within the bound.
A program may use at most 192 MiB of HBM per device.

```python
import jax
import jax.numpy as jnp
from jax import lax

D = 4096
LENGTH = 8192
BLOCK = 1024
SECTIONS = 2
N_CHAN = 4


def draw_channel_persistence(key, part):
    coin_key, slow_key, fast_key = jax.random.split(jax.random.fold_in(key, 11), 3)
    slow_share = 0.5
    slow = jax.random.uniform(coin_key, (D,), jnp.float32) < slow_share
    slow_rate = jnp.exp(jax.random.uniform(slow_key, (D,), jnp.float32, jnp.log(0.1 / LENGTH), jnp.log(2.0 / LENGTH)))
    fast_rate = jnp.exp(jax.random.uniform(fast_key, (D,), jnp.float32, jnp.log(1.0 / 512.0), jnp.log(1.0 / 30.0)))
    rates = jnp.where(slow, slow_rate, fast_rate)
    return jnp.exp(-rates).astype(jnp.float32)


def draw_position_boosts(key, part):
    place_key, depth_key = jax.random.split(jax.random.fold_in(key, 23), 2)
    hits = jax.random.uniform(place_key, (LENGTH,), jnp.float32) < 8.0 / LENGTH
    depth = jax.random.uniform(depth_key, (LENGTH,), jnp.float32, 0.5, 0.8)
    return jnp.where(hits, depth, 1.0).astype(jnp.float32)


def steps_of(stream_key, shape, shards, smallest, largest):
    level, own = 1.0, jax.random.fold_in(stream_key, 6)
    for dim, parts in shards:
        steps = jnp.exp(jax.random.uniform(jax.random.fold_in(own, dim), (parts,), jnp.float32, smallest / len(shards), largest / len(shards)))
        level = level * jnp.repeat(steps, shape[dim] // parts).reshape([-1 if axis == dim else 1 for axis in range(len(shape))])
    return level


def scatter_about(rng, extent, scale, limit, shards=(), dtype=jnp.bfloat16):
    values = scale * jax.random.normal(rng, extent, jnp.float32)
    if shards:
        values = values * steps_of(rng, extent, shards, -0.22, 0.18)
    return jnp.clip(values, -limit, limit).astype(dtype)


def setup_inputs(seed: int = 0) -> dict:
    splits = jax.random.split(jax.random.key(seed), 8)
    layer_source = scatter_about(splits[0], (LENGTH, D), 1.0, 6.0, ((0, 8), (1, 4)))
    entering_mixer_sections = scatter_about(splits[1], (SECTIONS, 2 * D, BLOCK), (2 * BLOCK) ** -0.5, 0.125, ((1, 4),))
    sigmoid_switch_matrix = scatter_about(splits[2], (D, BLOCK), BLOCK ** -0.5, 0.1875, ((0, 4),))
    leaving_mixer_sections = scatter_about(splits[3], (SECTIONS, 2 * D, BLOCK), (2 * BLOCK) ** -0.5, 0.125, ((1, 4),))
    channel_persistence = draw_channel_persistence(jax.random.fold_in(splits[7], 71), 0)
    position_boosts = draw_position_boosts(jax.random.fold_in(splits[7], 71), 0)
    result_cotangent = scatter_about(splits[6], (LENGTH, D), 1.0, 6.0, ((0, 8), (1, 4)))
    return {"layer_source": layer_source, "entering_mixer_sections": entering_mixer_sections, "sigmoid_switch_matrix": sigmoid_switch_matrix, "leaving_mixer_sections": leaving_mixer_sections, "channel_persistence": channel_persistence, "position_boosts": position_boosts, "result_cotangent": result_cotangent}


def link(earlier, following):
    return (earlier[0] * following[0], following[0] * earlier[1] + following[1])

def dot_rows(left, right):
    return lax.dot_general(left, right, (((0,), (0,)), ((), ())), preferred_element_type=jnp.float32)

def dot_trans(left, right):
    return lax.dot_general(left, right, (((1,), (1,)), ((), ())), preferred_element_type=jnp.float32)

def forward_map(blocks, weights, round_last):
    width = BLOCK
    stored = []
    for level in range(SECTIONS):
        stored.append(blocks)
        result = []
        for owner in range(N_CHAN):
            partner = owner ^ 1 << level
            local_w = weights[level, owner * 2 * width:(owner + 1) * 2 * width]
            summed = jnp.dot(blocks[owner], local_w[:width], preferred_element_type=jnp.float32)
            summed = summed + jnp.dot(blocks[partner], local_w[width:], preferred_element_type=jnp.float32)
            if round_last or level + 1 < SECTIONS:
                summed = summed.astype(jnp.bfloat16)
            result.append(summed)
        blocks = result
    return (blocks, stored)

def backward_map(cotans, weights, stored, round_last):
    width = BLOCK
    grads = [None] * SECTIONS
    for level in reversed(range(SECTIONS)):
        inputs = stored[level]
        shares = []
        for owner in range(N_CHAN):
            local_w = weights[level, owner * 2 * width:(owner + 1) * 2 * width]
            shares.append(dot_trans(cotans[owner], local_w[width:]).astype(jnp.bfloat16))
        result = []
        pieces = []
        for owner in range(N_CHAN):
            partner = owner ^ 1 << level
            local_w = weights[level, owner * 2 * width:(owner + 1) * 2 * width]
            own_grad = dot_rows(inputs[owner], cotans[owner])
            mate_grad = dot_rows(inputs[partner], cotans[owner])
            pieces.append(jnp.concatenate([own_grad, mate_grad], axis=0))
            summed = dot_trans(cotans[owner], local_w[:width]) + shares[partner].astype(jnp.float32)
            if round_last or level > 0:
                summed = summed.astype(jnp.bfloat16)
            result.append(summed)
        grads[level] = jnp.concatenate(pieces, axis=0)
        cotans = result
    return (cotans, jnp.stack(grads))

def reference(layer_source, entering_mixer_sections, sigmoid_switch_matrix, leaving_mixer_sections, channel_persistence, position_boosts, result_cotangent):
    width = BLOCK
    token_blocks = [layer_source[:, owner * width:(owner + 1) * width] for owner in range(N_CHAN)]
    grad_blocks = [result_cotangent[:, owner * width:(owner + 1) * width] for owner in range(N_CHAN)]
    drives, in_stored = forward_map(token_blocks, entering_mixer_sections, True)
    mixed_blocks = []
    saved = []
    for owner in range(N_CHAN):
        local_gate = sigmoid_switch_matrix[owner * width:(owner + 1) * width]
        gate = jax.nn.sigmoid(jnp.dot(token_blocks[owner], local_gate, preferred_element_type=jnp.float32))
        segment_shrink_multiplier = channel_persistence[owner * width:(owner + 1) * width]
        surviving_portion = segment_shrink_multiplier[None, :] * position_boosts[:, None]
        input_scale = jnp.sqrt(1.0 - segment_shrink_multiplier * segment_shrink_multiplier)
        drive = input_scale[None, :] * drives[owner].astype(jnp.float32)
        products, hidden = lax.associative_scan(link, (surviving_portion, drive))
        mixed_blocks.append((hidden * gate).astype(jnp.bfloat16))
        saved.append((gate, surviving_portion, input_scale, hidden))
    branches, out_stored = forward_map(mixed_blocks, leaving_mixer_sections, False)
    layer_out = jnp.concatenate([(token_blocks[owner].astype(jnp.float32) + branches[owner]).astype(jnp.bfloat16) for owner in range(N_CHAN)], axis=1)
    out_cots, out_sums = backward_map(grad_blocks, leaving_mixer_sections, out_stored, False)
    drive_grads = []
    gate_pres = []
    for owner in range(N_CHAN):
        gate, surviving_portion, input_scale, hidden = saved[owner]
        out_cot = out_cots[owner]
        hidden_grad = out_cot * gate
        gate_pre_grad = (out_cot * hidden * gate * (1.0 - gate)).astype(jnp.bfloat16)
        rev_prod, carried = lax.associative_scan(link, (surviving_portion, surviving_portion * hidden_grad), reverse=True)
        after = jnp.concatenate([carried[1:], jnp.zeros((1, width), jnp.float32)], axis=0)
        state_grad = hidden_grad + after
        drive_grads.append((input_scale[None, :] * state_grad).astype(jnp.bfloat16))
        gate_pres.append(gate_pre_grad)
    input_sides, in_sums = backward_map(drive_grads, entering_mixer_sections, in_stored, False)
    grad_scale = LENGTH ** (-0.5)
    token_parts = []
    gate_parts = []
    for owner in range(N_CHAN):
        local_gate = sigmoid_switch_matrix[owner * width:(owner + 1) * width]
        summed = grad_blocks[owner].astype(jnp.float32) + input_sides[owner] + dot_trans(gate_pres[owner], local_gate)
        token_parts.append(summed.astype(jnp.bfloat16))
        gate_parts.append(dot_rows(token_blocks[owner], gate_pres[owner]))
    token_grads = jnp.concatenate(token_parts, axis=1)
    gate_grads = jnp.concatenate(gate_parts, axis=0) * grad_scale
    return (layer_out, token_grads, in_sums * grad_scale, out_sums * grad_scale, gate_grads)
```

```python
import functools

import jax
import jax.numpy as jnp
from jax import lax
from jax.experimental import pallas as pl
from jax.experimental.pallas import tpu as pltpu
from jax.sharding import PartitionSpec as P

SEGMENTS = 32
LANES = 128


def from_partner(block, axis, distance):
    count = lax.axis_size(axis)
    route = []
    for low in range(count):
        high = low | 1 << distance
        if high != low and high < count:
            route += [(low, high), (high, low)]
    return lax.ppermute(block, axis, route)


def dot(left, right):
    return jnp.dot(left, right, preferred_element_type=jnp.float32)


def dot_rows(left, right):
    return lax.dot_general(
        left, right, (((0,), (0,)), ((), ())), preferred_element_type=jnp.float32
    )


def dot_trans(left, right):
    return lax.dot_general(
        left, right, (((1,), (1,)), ((), ())), preferred_element_type=jnp.float32
    )


def every(ref, step):
    return ref[pl.ds(step, SEGMENTS, stride=ref.shape[0] // SEGMENTS), :]


def ends_kernel(drive, out_cot, gate, keep, boosts, seg_ref, tot_ref, x_ref, g_ref):
    lam = keep[...]
    scale = jnp.sqrt(1.0 - lam * lam)
    x_ref[...] = scale * drive[...].astype(jnp.float32)
    g_ref[...] = out_cot[...] * gate[...]
    steps = x_ref.shape[0] // SEGMENTS
    shape = (SEGMENTS, LANES)
    lam = jnp.broadcast_to(lam, shape)
    state = jnp.zeros(shape, jnp.float32)
    prod = jnp.ones(shape, jnp.float32)
    for i in range(steps):
        a = every(boosts, i) * lam
        state = a * state + every(x_ref, i)
        prod = a * prod
    back = jnp.zeros(shape, jnp.float32)
    for i in reversed(range(steps)):
        a = every(boosts, i) * lam
        back = a * (every(g_ref, i) + back)
    seg_ref[0] = prod
    seg_ref[1] = state
    seg_ref[2] = back
    p = jnp.ones((1, LANES), jnp.float32)
    h = jnp.zeros((1, LANES), jnp.float32)
    c = jnp.zeros((1, LANES), jnp.float32)
    for s in range(SEGMENTS):
        here = prod[s : s + 1]
        h = here * h + state[s : s + 1]
        p = here * p
        r = SEGMENTS - 1 - s
        c = prod[r : r + 1] * c + back[r : r + 1]
    tot_ref[0] = p
    tot_ref[1] = h
    tot_ref[2] = c


def run_kernel(
    devices, drive, out_cot, gate, keep, boosts, seg, tots, place,
    mixed, gate_pre, drive_grad, x_ref, g_ref, start_ref, stop_ref,
):
    lam = keep[...]
    scale = jnp.sqrt(1.0 - lam * lam)
    x_ref[...] = scale * drive[...].astype(jnp.float32)
    g_ref[...] = out_cot[...] * gate[...]
    steps = x_ref.shape[0] // SEGMENTS
    shape = (SEGMENTS, LANES)
    here = place[...]
    h = jnp.zeros((1, LANES), jnp.float32)
    c = jnp.zeros((1, LANES), jnp.float32)
    for k in range(devices):
        h = jnp.where(k < here, tots[k, 0] * h + tots[k, 1], h)
        r = devices - 1 - k
        c = jnp.where(r > here, tots[r, 0] * c + tots[r, 2], c)
    for s in range(SEGMENTS):
        start_ref[s : s + 1] = h
        h = seg[0, s : s + 1] * h + seg[1, s : s + 1]
        r = SEGMENTS - 1 - s
        stop_ref[r : r + 1] = c
        c = seg[0, r : r + 1] * c + seg[2, r : r + 1]
    lam = jnp.broadcast_to(lam, shape)
    state = start_ref[...]
    back = stop_ref[...]
    for i in range(steps):
        state = every(boosts, i) * lam * state + every(x_ref, i)
        x_ref[pl.ds(i, SEGMENTS, stride=steps), :] = state
        r = steps - 1 - i
        total = every(g_ref, r) + back
        g_ref[pl.ds(r, SEGMENTS, stride=steps), :] = total
        back = every(boosts, r) * lam * total
    sig = gate[...]
    product = x_ref[...] * sig
    mixed[...] = product.astype(jnp.bfloat16)
    gate_pre[...] = (out_cot[...] * product * (1.0 - sig)).astype(jnp.bfloat16)
    drive_grad[...] = (scale * g_ref[...]).astype(jnp.bfloat16)


def recurrences(drive, out_cot, gate, keep, boosts):
    tokens, width = drive.shape
    devices = lax.axis_size("seq")
    keep = keep[None, :]
    boosts = jnp.broadcast_to(boosts[:, None], (tokens, LANES))
    big = pl.BlockSpec((tokens, LANES), lambda j: (0, j))
    row = pl.BlockSpec((1, LANES), lambda j: (0, j))
    same = pl.BlockSpec((tokens, LANES), lambda j: (0, 0))
    seg_spec = pl.BlockSpec((3, SEGMENTS, LANES), lambda j: (0, 0, j))
    scratch = pltpu.VMEM((tokens, LANES), jnp.float32)
    small = pltpu.VMEM((SEGMENTS, LANES), jnp.float32)
    area = tokens * width
    seg, totals = pl.pallas_call(
        ends_kernel,
        grid=(width // LANES,),
        in_specs=[big, big, big, row, same],
        out_specs=[seg_spec, pl.BlockSpec((3, 1, LANES), lambda j: (0, 0, j))],
        out_shape=[
            jax.ShapeDtypeStruct((3, SEGMENTS, width), jnp.float32),
            jax.ShapeDtypeStruct((3, 1, width), jnp.float32),
        ],
        scratch_shapes=[scratch, scratch],
        compiler_params=pltpu.CompilerParams(vmem_limit_bytes=24 << 20),
        cost_estimate=pl.CostEstimate(flops=10 * area, bytes_accessed=10 * area, transcendentals=0),
        name="ends",
    )(drive, out_cot, gate, keep, boosts)
    totals = lax.all_gather(totals, "seq")
    place = jnp.full((1, LANES), lax.axis_index("seq"), jnp.int32)
    return pl.pallas_call(
        functools.partial(run_kernel, devices),
        grid=(width // LANES,),
        in_specs=[
            big, big, big, row, same, seg_spec,
            pl.BlockSpec((devices, 3, 1, LANES), lambda j: (0, 0, 0, j)),
            pl.BlockSpec((1, LANES), lambda j: (0, 0)),
        ],
        out_specs=[big, big, big],
        out_shape=[jax.ShapeDtypeStruct((tokens, width), jnp.bfloat16)] * 3,
        scratch_shapes=[scratch, scratch, small, small],
        compiler_params=pltpu.CompilerParams(vmem_limit_bytes=24 << 20),
        cost_estimate=pl.CostEstimate(flops=20 * area, bytes_accessed=16 * area, transcendentals=0),
        name="recurrences",
    )(drive, out_cot, gate, keep, boosts, seg, totals, place)


def share_of(cotangent, weight):
    return dot_trans(cotangent, weight[cotangent.shape[1] :]).astype(jnp.bfloat16)


def transposed_step(cotangent, weight, received):
    width = cotangent.shape[1]
    return dot_trans(cotangent, weight[:width]) + received.astype(jnp.float32)


def weight_grad(own, partner, cotangent, scale):
    both = jnp.concatenate(
        [
            dot_rows(own, cotangent).astype(jnp.bfloat16),
            dot_rows(partner, cotangent).astype(jnp.bfloat16),
        ],
        axis=0,
    )
    part = lax.psum_scatter(both, "seq", scatter_dimension=0, tiled=True)
    return part.astype(jnp.float32) * scale


def shards(
    layer_source,
    entering,
    switch,
    leaving,
    channel_persistence,
    position_boosts,
    result_cotangent,
):
    levels = entering.shape[0]
    width = layer_source.shape[1]
    scale = float(layer_source.shape[0] * lax.axis_size("seq")) ** (-0.5)

    z, z_mates = [layer_source], []
    e = [None] * levels + [result_cotangent]
    for step in range(levels):
        z_mates.append(from_partner(z[step], "chan", step))
        down = levels - 1 - step
        share = from_partner(share_of(e[down + 1], leaving[down]), "chan", down)
        e[down] = transposed_step(e[down + 1], leaving[down], share)
        if down > 0:
            e[down] = e[down].astype(jnp.bfloat16)
        summed = dot(z[step], entering[step, :width]) + dot(z_mates[step], entering[step, width:])
        z.append(summed.astype(jnp.bfloat16))
    gate = jax.nn.sigmoid(dot(layer_source, switch))

    mixed, gate_pre_grad, drive_grad = recurrences(
        z[levels], e[0], gate, channel_persistence, position_boosts
    )

    w, w_mates = [mixed], []
    f = [None] * levels + [drive_grad]
    in_grads, out_grads = [None] * levels, [None] * levels
    for step in range(levels):
        down = levels - 1 - step
        held = gate_pre_grad if step == 0 else w_mates[step - 1]
        share, sent, ready, held = lax.optimization_barrier(
            (share_of(f[down + 1], entering[down]), w[step], f[down + 1], held)
        )
        share = from_partner(share, "chan", down)
        mate = from_partner(sent, "chan", step)
        if step == 0:
            gate_pre_grad = held
            gate_sum = lax.psum_scatter(
                dot_rows(layer_source, gate_pre_grad).astype(jnp.bfloat16),
                "seq", scatter_dimension=0, tiled=True,
            )
        else:
            out_grads[step - 1] = weight_grad(w[step - 1], held, e[step], scale)
        in_grads[down] = weight_grad(z[down], z_mates[down], ready, scale)
        mate, share = lax.optimization_barrier((mate, share))
        w_mates.append(mate)
        f[down] = transposed_step(f[down + 1], entering[down], share)
        if down > 0:
            f[down] = f[down].astype(jnp.bfloat16)
        summed = dot(w[step], leaving[step, :width]) + dot(mate, leaving[step, width:])
        if step + 1 < levels:
            summed = summed.astype(jnp.bfloat16)
        w.append(summed)
    out_grads[levels - 1] = weight_grad(w[levels - 1], w_mates[levels - 1], e[levels], scale)
    layer_out = (layer_source.astype(jnp.float32) + w[levels]).astype(jnp.bfloat16)
    token_grads = (
        result_cotangent.astype(jnp.float32) + f[0] + dot_trans(gate_pre_grad, switch)
    ).astype(jnp.bfloat16)
    return (
        layer_out,
        token_grads,
        jnp.stack(in_grads),
        jnp.stack(out_grads),
        gate_sum.astype(jnp.float32) * scale,
    )


def solution(mesh):
    placed = (
        P("seq", "chan"),
        P(None, "chan", None),
        P("chan", None),
        P(None, "chan", None),
        P("chan"),
        P("seq"),
        P("seq", "chan"),
    )
    return jax.shard_map(
        shards,
        mesh=mesh,
        in_specs=placed,
        out_specs=(
            P("seq", "chan"),
            P("seq", "chan"),
            P(None, ("chan", "seq"), None),
            P(None, ("chan", "seq"), None),
            P(("chan", "seq"), None),
        ),
        check_vma=False,
    )
```

```python
import functools

import jax
import jax.numpy as jnp
from jax import lax
from jax.experimental import pallas as pl
from jax.experimental.pallas import tpu as pltpu
from jax.sharding import PartitionSpec as P

SEGMENTS = 32
LANES = 128


def from_partner(block, axis, distance):
    count = lax.axis_size(axis)
    route = []
    for low in range(count):
        high = low | 1 << distance
        if high != low and high < count:
            route += [(low, high), (high, low)]
    return lax.ppermute(block, axis, route)


def dot(left, right):
    return jnp.dot(left, right, preferred_element_type=jnp.float32)


def dot_rows(left, right):
    return lax.dot_general(
        left, right, (((0,), (0,)), ((), ())), preferred_element_type=jnp.float32
    )


def dot_trans(left, right):
    return lax.dot_general(
        left, right, (((1,), (1,)), ((), ())), preferred_element_type=jnp.float32
    )


def every(ref, step):
    return ref[pl.ds(step, SEGMENTS, stride=ref.shape[0] // SEGMENTS), :]


def ends_kernel(drive, out_cot, gate, keep, boosts, seg_ref, tot_ref, x_ref, g_ref):
    lam = keep[...]
    scale = jnp.sqrt(1.0 - lam * lam)
    x_ref[...] = scale * drive[...].astype(jnp.float32)
    g_ref[...] = out_cot[...] * gate[...]
    steps = x_ref.shape[0] // SEGMENTS
    shape = (SEGMENTS, LANES)
    lam = jnp.broadcast_to(lam, shape)
    state = jnp.zeros(shape, jnp.float32)
    prod = jnp.ones(shape, jnp.float32)
    for i in range(steps):
        a = every(boosts, i) * lam
        state = a * state + every(x_ref, i)
        prod = a * prod
    back = jnp.zeros(shape, jnp.float32)
    for i in reversed(range(steps)):
        a = every(boosts, i) * lam
        back = a * (every(g_ref, i) + back)
    seg_ref[0] = prod
    seg_ref[1] = state
    seg_ref[2] = back
    p = jnp.ones((1, LANES), jnp.float32)
    h = jnp.zeros((1, LANES), jnp.float32)
    c = jnp.zeros((1, LANES), jnp.float32)
    for s in range(SEGMENTS):
        here = prod[s : s + 1]
        h = here * h + state[s : s + 1]
        p = here * p
        r = SEGMENTS - 1 - s
        c = prod[r : r + 1] * c + back[r : r + 1]
    tot_ref[0] = p
    tot_ref[1] = h
    tot_ref[2] = c


def run_kernel(
    devices, drive, out_cot, gate, keep, boosts, seg, tots, place,
    mixed, gate_pre, drive_grad, x_ref, g_ref, start_ref, stop_ref,
):
    lam = keep[...]
    scale = jnp.sqrt(1.0 - lam * lam)
    x_ref[...] = scale * drive[...].astype(jnp.float32)
    g_ref[...] = out_cot[...] * gate[...]
    steps = x_ref.shape[0] // SEGMENTS
    shape = (SEGMENTS, LANES)
    here = place[...]
    h = jnp.zeros((1, LANES), jnp.float32)
    c = jnp.zeros((1, LANES), jnp.float32)
    for k in range(devices):
        h = jnp.where(k < here, tots[k, 0] * h + tots[k, 1], h)
        r = devices - 1 - k
        c = jnp.where(r > here, tots[r, 0] * c + tots[r, 2], c)
    for s in range(SEGMENTS):
        start_ref[s : s + 1] = h
        h = seg[0, s : s + 1] * h + seg[1, s : s + 1]
        r = SEGMENTS - 1 - s
        stop_ref[r : r + 1] = c
        c = seg[0, r : r + 1] * c + seg[2, r : r + 1]
    lam = jnp.broadcast_to(lam, shape)
    state = start_ref[...]
    back = stop_ref[...]
    for i in range(steps):
        state = every(boosts, i) * lam * state + every(x_ref, i)
        x_ref[pl.ds(i, SEGMENTS, stride=steps), :] = state
        r = steps - 1 - i
        total = every(g_ref, r) + back
        g_ref[pl.ds(r, SEGMENTS, stride=steps), :] = total
        back = every(boosts, r) * lam * total
    sig = gate[...]
    product = x_ref[...] * sig
    mixed[...] = product.astype(jnp.bfloat16)
    gate_pre[...] = (out_cot[...] * product * (1.0 - sig)).astype(jnp.bfloat16)
    drive_grad[...] = (scale * g_ref[...]).astype(jnp.bfloat16)


def recurrences(drive, out_cot, gate, keep, boosts):
    tokens, width = drive.shape
    devices = lax.axis_size("seq")
    keep = keep[None, :]
    boosts = jnp.broadcast_to(boosts[:, None], (tokens, LANES))
    big = pl.BlockSpec((tokens, LANES), lambda j: (0, j))
    row = pl.BlockSpec((1, LANES), lambda j: (0, j))
    same = pl.BlockSpec((tokens, LANES), lambda j: (0, 0))
    seg_spec = pl.BlockSpec((3, SEGMENTS, LANES), lambda j: (0, 0, j))
    scratch = pltpu.VMEM((tokens, LANES), jnp.float32)
    small = pltpu.VMEM((SEGMENTS, LANES), jnp.float32)
    area = tokens * width
    seg, totals = pl.pallas_call(
        ends_kernel,
        grid=(width // LANES,),
        in_specs=[big, big, big, row, same],
        out_specs=[seg_spec, pl.BlockSpec((3, 1, LANES), lambda j: (0, 0, j))],
        out_shape=[
            jax.ShapeDtypeStruct((3, SEGMENTS, width), jnp.float32),
            jax.ShapeDtypeStruct((3, 1, width), jnp.float32),
        ],
        scratch_shapes=[scratch, scratch],
        compiler_params=pltpu.CompilerParams(vmem_limit_bytes=24 << 20),
        cost_estimate=pl.CostEstimate(flops=10 * area, bytes_accessed=10 * area, transcendentals=0),
        name="ends",
    )(drive, out_cot, gate, keep, boosts)
    totals = lax.all_gather(totals, "seq")
    place = jnp.full((1, LANES), lax.axis_index("seq"), jnp.int32)
    return pl.pallas_call(
        functools.partial(run_kernel, devices),
        grid=(width // LANES,),
        in_specs=[
            big, big, big, row, same, seg_spec,
            pl.BlockSpec((devices, 3, 1, LANES), lambda j: (0, 0, 0, j)),
            pl.BlockSpec((1, LANES), lambda j: (0, 0)),
        ],
        out_specs=[big, big, big],
        out_shape=[jax.ShapeDtypeStruct((tokens, width), jnp.bfloat16)] * 3,
        scratch_shapes=[scratch, scratch, small, small],
        compiler_params=pltpu.CompilerParams(vmem_limit_bytes=24 << 20),
        cost_estimate=pl.CostEstimate(flops=20 * area, bytes_accessed=16 * area, transcendentals=0),
        name="recurrences",
    )(drive, out_cot, gate, keep, boosts, seg, totals, place)


def share_of(cotangent, weight):
    return dot_trans(cotangent, weight[cotangent.shape[1] :]).astype(jnp.bfloat16)


def transposed_step(cotangent, weight, received):
    width = cotangent.shape[1]
    return dot_trans(cotangent, weight[:width]) + received.astype(jnp.float32)


def halved(part, distance):
    count = lax.axis_size("seq")
    width = part.shape[1]
    pairs = part.reshape(count // (2 * distance), 2, -1, width)
    mine = (lax.axis_index("seq") // distance) % 2
    kept = lax.dynamic_index_in_dim(pairs, mine, 1, keepdims=False)
    sent = lax.dynamic_index_in_dim(pairs, 1 - mine, 1, keepdims=False)
    got = lax.ppermute(sent, "seq", [(i, i ^ distance) for i in range(count)])
    return (kept.astype(jnp.float32) + got.astype(jnp.float32)).reshape(-1, width)


def further(part, distance, stop):
    while distance < stop:
        part = halved(part.astype(jnp.bfloat16), distance)
        distance *= 2
    return part if stop == lax.axis_size("seq") else part.astype(jnp.bfloat16)


def local_grad(own, partner, cotangent):
    return jnp.concatenate(
        [
            dot_rows(own, cotangent).astype(jnp.bfloat16),
            dot_rows(partner, cotangent).astype(jnp.bfloat16),
        ],
        axis=0,
    )


def weight_grad(own, partner, cotangent, scale):
    both = local_grad(own, partner, cotangent)
    part = lax.psum_scatter(both, "seq", scatter_dimension=0, tiled=True)
    return part.astype(jnp.float32) * scale


def shards(
    layer_source,
    entering,
    switch,
    leaving,
    channel_persistence,
    position_boosts,
    result_cotangent,
):
    levels = entering.shape[0]
    width = layer_source.shape[1]
    scale = float(layer_source.shape[0] * lax.axis_size("seq")) ** (-0.5)

    z, z_mates = [layer_source], []
    e = [None] * levels + [result_cotangent]
    for step in range(levels):
        z_mates.append(from_partner(z[step], "chan", step))
        down = levels - 1 - step
        share = from_partner(share_of(e[down + 1], leaving[down]), "chan", down)
        e[down] = transposed_step(e[down + 1], leaving[down], share)
        if down > 0:
            e[down] = e[down].astype(jnp.bfloat16)
        summed = dot(z[step], entering[step, :width]) + dot(z_mates[step], entering[step, width:])
        z.append(summed.astype(jnp.bfloat16))
    gate = jax.nn.sigmoid(dot(layer_source, switch))

    mixed, gate_pre_grad, drive_grad = recurrences(
        z[levels], e[0], gate, channel_persistence, position_boosts
    )

    w, w_mates = [mixed], []
    f = [None] * levels + [drive_grad]
    in_grads, out_grads = [None] * levels, [None] * levels
    parts, done_to = {}, {}
    for step in range(levels):
        down = levels - 1 - step
        held = gate_pre_grad if step == 0 else w_mates[step - 1]
        share, sent, ready, held = lax.optimization_barrier(
            (share_of(f[down + 1], entering[down]), w[step], f[down + 1], held)
        )
        share = from_partner(share, "chan", down)
        mate = from_partner(sent, "chan", step)
        if step == 0:
            gate_pre_grad = held
            gate_sum = lax.psum_scatter(
                dot_rows(layer_source, gate_pre_grad).astype(jnp.bfloat16),
                "seq", scatter_dimension=0, tiled=True,
            )
        else:
            out_grads[step - 1] = weight_grad(w[step - 1], held, e[step], scale)
        parts[down] = local_grad(z[down], z_mates[down], ready)
        early = {}
        if step > 0:
            early[down + 1] = further(parts[down + 1], 1, 4)
        if step + 1 == levels:
            early[down] = further(parts[down], 1, 2)
        mate, share, early = lax.optimization_barrier((mate, share, early))
        for at, part in early.items():
            parts[at] = part
            done_to[at] = 4 if at > down else 2
        w_mates.append(mate)
        f[down] = transposed_step(f[down + 1], entering[down], share)
        if down > 0:
            f[down] = f[down].astype(jnp.bfloat16)
        summed = dot(w[step], leaving[step, :width]) + dot(mate, leaving[step, width:])
        if step + 1 < levels:
            summed = summed.astype(jnp.bfloat16)
        w.append(summed)
    for at in range(levels):
        start = 1 if at not in done_to else done_to[at]
        in_grads[at] = further(parts[at], start, lax.axis_size("seq")).astype(jnp.float32) * scale
    out_grads[levels - 1] = weight_grad(w[levels - 1], w_mates[levels - 1], e[levels], scale)
    layer_out = (layer_source.astype(jnp.float32) + w[levels]).astype(jnp.bfloat16)
    token_grads = (
        result_cotangent.astype(jnp.float32) + f[0] + dot_trans(gate_pre_grad, switch)
    ).astype(jnp.bfloat16)
    return (
        layer_out,
        token_grads,
        jnp.stack(in_grads),
        jnp.stack(out_grads),
        gate_sum.astype(jnp.float32) * scale,
    )


def solution(mesh):
    placed = (
        P("seq", "chan"),
        P(None, "chan", None),
        P("chan", None),
        P(None, "chan", None),
        P("chan"),
        P("seq"),
        P("seq", "chan"),
    )
    return jax.shard_map(
        shards,
        mesh=mesh,
        in_specs=placed,
        out_specs=(
            P("seq", "chan"),
            P("seq", "chan"),
            P(None, ("chan", "seq"), None),
            P(None, ("chan", "seq"), None),
            P(("chan", "seq"), None),
        ),
        check_vma=False,
    )
```
